128 devices in a mesh: tm: 8 (over y, core), expert: 16 (over z, x).
Axes of the slice: x: 4, y: 4, z: 4, core: 2. Of those that a mesh axis runs over, the one named last changes fastest.
Arguments:
- queries: bfloat16 [16384, 2048], P(('tm', 'expert')), may hold values from -6 to 6
- keys: bfloat16 [16384, 2048], P(('tm', 'expert')), may hold values from -6 to 6
- values: bfloat16 [16384, 2048], P(('tm', 'expert')), may hold values from -6 to 6
- out_grad: bfloat16 [16384, 2048], P(('tm', 'expert')), may hold values from -6 to 6
- expert_ids: int32 [16384, 2], P(('tm', 'expert')), may hold values from 0 to 31, all different within a row
- combine_gates: float32 [16384, 2], P(('tm', 'expert')), may hold values from 0.2 to 1
- gate_weight: bfloat16 [128, 2048, 512], P(('tm', 'expert')), may hold values from -0.125 to 0.125
- up_weight: bfloat16 [128, 2048, 512], P(('tm', 'expert')), may hold values from -0.125 to 0.125
- down_weight: bfloat16 [128, 512, 2048], P(('tm', 'expert')), may hold values from -0.125 to 0.125
Outputs:
- query_grad: bfloat16 [16384, 2048], P(('tm', 'expert'))
- key_grad: bfloat16 [16384, 2048], P(('tm', 'expert'))
- value_grad: bfloat16 [16384, 2048], P(('tm', 'expert'))
- gate_weight_grad: float32 [128, 2048, 512], P(('tm', 'expert'))
- up_weight_grad: float32 [128, 2048, 512], P(('tm', 'expert'))
- down_weight_grad: float32 [128, 512, 2048], P(('tm', 'expert'))
The draws below stay inside these ranges and needn't reach their ends.
Inputs may be any that keep to these rules, and one draw needn't show every extreme that they name: `expert_ids`: the two experts of a token differ.
All inputs are finite; a program needn't handle non-finite values.
Results may differ from the reference program's by a relative error of at most 0.017.
Values may be sent and summed in bfloat16 or wider, within the bound.
A program may use at most 192 MiB of HBM per device.

```python
import jax
import jax.numpy as jnp
from jax import lax

HEADS = 16
HEAD_DIM = 128
D = 2048
FF = 2048
SLICES = 4
TOK_DEV = 128
EXPERTS = 32
CAP = 12
TOKENS = 16384
N_TM = 8
N_EXPERT = 16
DEVICES = 128


def level_of(stream_key, extent, pieces, smallest, top_value):
    def one(axis_at, shards_of):
        draws = jax.random.uniform(jax.random.fold_in(jax.random.fold_in(stream_key, 6), axis_at), (shards_of,), jnp.float32, smallest / len(pieces), top_value / len(pieces))
        return jnp.repeat(jnp.exp(draws), extent[axis_at] // shards_of).reshape((-1,) + (1,) * (len(extent) - axis_at - 1))

    level = one(*pieces[0])
    for cut in pieces[1:]:
        level = level * one(*cut)
    return level


def choose_distinct(rng, rows, amount, top, lift):
    order = jax.random.permutation(jax.random.fold_in(rng, 1), amount)
    pull = order
    for power in range(3):
        pull = pull * pull // amount
    pull = pull * lift // amount
    lots = jax.random.randint(jax.random.fold_in(rng, 2), (rows, amount), 0, 4096) + pull
    sure = jax.random.permutation(jax.random.fold_in(rng, 3), rows)[jnp.arange(amount) % rows]
    lots = jnp.where(jnp.arange(rows)[:, None] == sure[None, :], 1 << 14, lots)
    score = lots * amount + jnp.arange(amount)
    return lax.top_k(score.astype(jnp.int32), top)[1].astype(jnp.int32)


def gaussian(own_key, extent, scale, reach, split=(), kind=jnp.bfloat16):
    drawn = scale * jax.random.normal(own_key, extent, jnp.float32)
    if split:
        drawn = drawn * level_of(own_key, extent, split, -0.22, 0.18)
    return jnp.clip(drawn, -reach, reach).astype(kind)


def setup_inputs(seed: int = 0) -> dict:
    streams_of = jax.random.split(jax.random.key(seed), 10)
    queries = gaussian(streams_of[0], (TOKENS, D), 1.0, 6.0, ((0, 128),))
    keys = gaussian(streams_of[1], (TOKENS, D), 1.0, 6.0, ((0, 128),))
    values = gaussian(streams_of[2], (TOKENS, D), 1.0, 6.0, ((0, 128),))
    out_grad = gaussian(streams_of[3], (TOKENS, D), 1.0, 6.0, ((0, 128),))
    expert_ids = choose_distinct(streams_of[4], TOKENS, EXPERTS, 2, 1024)
    combine_gates = jnp.clip(0.2 + 0.8 * jax.random.uniform(streams_of[5], (TOKENS, 2), jnp.float32) ** level_of(streams_of[5], (TOKENS, 2), ((0, 128),), -0.2, 0.2), 0.2, 1.0)
    gate_weight = gaussian(streams_of[6], (EXPERTS * SLICES, D, FF // SLICES), D ** -0.5, 0.125, ((0, 128),))
    up_weight = gaussian(streams_of[7], (EXPERTS * SLICES, D, FF // SLICES), D ** -0.5, 0.125, ((0, 128),))
    down_weight = gaussian(streams_of[8], (EXPERTS * SLICES, FF // SLICES, D), FF ** -0.5, 0.125, ((0, 128),))
    return dict(queries=queries, keys=keys, values=values, out_grad=out_grad, expert_ids=expert_ids, combine_gates=combine_gates, gate_weight=gate_weight, up_weight=up_weight, down_weight=down_weight)


epsilon = 1e-06
highest = lax.Precision.HIGHEST

def slot_places(routes, capacity, experts):
    flat_ids = routes.reshape(-1).astype(jnp.int32)
    onehot = (flat_ids[:, None] == jnp.arange(experts, dtype=jnp.int32)[None, :]).astype(jnp.int32)
    earlier = jnp.cumsum(onehot, axis=0) - onehot
    position = lax.optimization_barrier(jnp.sum(earlier * onehot, axis=1))
    return jnp.where(position < capacity, flat_ids * capacity + position, experts * capacity).astype(jnp.int32)

def expert_slice(rows, grad_rows, gate_part, up_part, down_part):
    gate = jnp.dot(rows, gate_part, preferred_element_type=jnp.float32)
    upper = jnp.dot(rows, up_part, preferred_element_type=jnp.float32)
    sigma = jax.nn.sigmoid(gate)
    act = (gate * sigma * upper).astype(jnp.bfloat16)
    act_grad = jnp.dot(grad_rows, down_part.T, preferred_element_type=jnp.float32)
    down_grad = jnp.dot(act.T, grad_rows, preferred_element_type=jnp.float32)
    gate_grad = (act_grad * upper * sigma * (1.0 + gate * (1.0 - sigma))).astype(jnp.bfloat16)
    up_grad = (act_grad * gate * sigma).astype(jnp.bfloat16)
    gate_wgrad = jnp.dot(rows.T, gate_grad, preferred_element_type=jnp.float32)
    up_wgrad = jnp.dot(rows.T, up_grad, preferred_element_type=jnp.float32)
    partial_sum = jnp.dot(gate_grad, gate_part.T, preferred_element_type=jnp.float32)
    partial_sum = partial_sum + jnp.dot(up_grad, up_part.T, preferred_element_type=jnp.float32)
    return (partial_sum.astype(jnp.bfloat16), gate_wgrad, up_wgrad, down_grad)

def reference(queries, keys, values, out_grad, expert_ids, combine_gates, gate_weight, up_weight, down_weight):
    per_span = TOK_DEV * N_EXPERT
    shape4 = (N_TM, per_span, HEADS, HEAD_DIM)
    query_f = queries.astype(jnp.float32).reshape(shape4)
    key_f = keys.astype(jnp.float32).reshape(shape4)
    value_f = values.astype(jnp.float32).reshape(shape4)
    local = jnp.einsum('ctha,cthb->chab', key_f, value_f, precision=highest)
    states = jnp.cumsum(local, axis=0)
    mixed = jnp.einsum('ctha,chab->cthb', query_f, states, precision=highest)
    scale = lax.rsqrt(lax.optimization_barrier(jnp.mean(mixed * mixed, axis=-1, keepdims=True)) + epsilon)
    normed = mixed * scale
    hidden = normed.astype(jnp.bfloat16).reshape(TOKENS, D)
    routes = expert_ids.reshape(DEVICES, TOK_DEV, 2)
    places = jax.vmap(lambda route: slot_places(route, CAP, EXPERTS))(routes)
    rows_h = jnp.repeat(hidden.reshape(DEVICES, TOK_DEV, D), 2, axis=1)
    rows_g = jnp.repeat(out_grad.astype(jnp.float32).reshape(DEVICES, TOK_DEV, D), 2, axis=1)
    rows_g = (rows_g * combine_gates.reshape(DEVICES, 2 * TOK_DEV, 1)).astype(jnp.bfloat16)

    def fill_rows(place, rows):
        return jnp.zeros((EXPERTS * CAP, D), jnp.bfloat16).at[place].set(rows, mode='drop')
    buffer_h = jax.vmap(fill_rows)(places, rows_h).reshape(DEVICES, EXPERTS, CAP, D)
    buffer_g = jax.vmap(fill_rows)(places, rows_g).reshape(DEVICES, EXPERTS, CAP, D)
    token_index = (jnp.arange(DEVICES * 2 * TOK_DEV, dtype=jnp.int32) // 2).reshape(DEVICES, 2 * TOK_DEV)

    def fill_index(place, index_row):
        return jnp.full((EXPERTS * CAP,), TOKENS, jnp.int32).at[place].set(index_row, mode='drop')
    slot_token = jax.vmap(fill_index)(places, token_index).reshape(DEVICES, EXPERTS, CAP)
    width_slice = FF // SLICES
    gate_all = gate_weight.reshape(EXPERTS, SLICES, D, width_slice)
    up_all = up_weight.reshape(EXPERTS, SLICES, D, width_slice)
    down_all = down_weight.reshape(EXPERTS, SLICES, width_slice, D)

    def per_expert(carry, inputs):
        rows_in, grads_in, tokens_in, gate_e, up_e, down_e = inputs
        rows = rows_in.reshape(DEVICES * CAP, D)
        grad_rows = grads_in.reshape(DEVICES * CAP, D)
        total = jnp.zeros((DEVICES * CAP, D), jnp.float32)
        gate_list, up_list, down_list = ([], [], [])
        for slice_index in range(SLICES):
            partial_sum, gate_wgrad, up_wgrad, down_grad = expert_slice(rows, grad_rows, gate_e[slice_index], up_e[slice_index], down_e[slice_index])
            total = total + partial_sum.astype(jnp.float32)
            gate_list.append(gate_wgrad)
            up_list.append(up_wgrad)
            down_list.append(down_grad)
        carry = carry.at[tokens_in.reshape(-1)].add(total, mode='drop')
        return (carry, (jnp.stack(gate_list), jnp.stack(up_list), jnp.stack(down_list)))
    moe_grad, stacked = lax.scan(per_expert, jnp.zeros((TOKENS, D), jnp.float32), (jnp.transpose(buffer_h, (1, 0, 2, 3)), jnp.transpose(buffer_g, (1, 0, 2, 3)), jnp.transpose(slot_token, (1, 0, 2)), gate_all, up_all, down_all))
    gate_weight_grad = stacked[0].reshape(EXPERTS * SLICES, D, width_slice)
    up_weight_grad = stacked[1].reshape(EXPERTS * SLICES, D, width_slice)
    down_weight_grad = stacked[2].reshape(EXPERTS * SLICES, width_slice, D)
    hidden_grad = (out_grad.astype(jnp.float32) + moe_grad).reshape(shape4)
    norm_grad = scale * (hidden_grad - normed * lax.optimization_barrier(jnp.mean(hidden_grad * normed, axis=-1, keepdims=True)))
    query_grad = jnp.einsum('cthb,chab->ctha', norm_grad, states, precision=highest)
    local_back = jnp.einsum('ctha,cthb->chab', query_f, norm_grad, precision=highest)
    back_states = jnp.flip(jnp.cumsum(jnp.flip(local_back, 0), axis=0), 0)
    key_grad = jnp.einsum('cthb,chab->ctha', value_f, back_states, precision=highest)
    value_grad = jnp.einsum('ctha,chab->cthb', key_f, back_states, precision=highest)
    return (query_grad.reshape(TOKENS, D).astype(jnp.bfloat16), key_grad.reshape(TOKENS, D).astype(jnp.bfloat16), value_grad.reshape(TOKENS, D).astype(jnp.bfloat16), gate_weight_grad, up_weight_grad, down_weight_grad)
```

```python
import functools

import jax
import jax.numpy as jnp
from jax import lax
from jax.experimental import pallas as pl
from jax.experimental.pallas import tpu as pltpu
from jax.sharding import PartitionSpec as P

MESH = pl.DeviceIdType.MESH
EPS = 1e-06
TOK = 128
HD = 128
CAP = 12
G = 4 * CAP
NE = 32
ROWS = NE * G
CH = 8 * G
BC = 512
D = 2048
HID = 512
DY = (0, 1, 3, 2)
BF = jnp.bfloat16
F32 = jnp.float32


def nn(a, b):
    return lax.dot_general(a, b, (((1,), (0,)), ((), ())), preferred_element_type=F32)


def nt(a, b):
    return lax.dot_general(a, b, (((1,), (1,)), ((), ())), preferred_element_type=F32)


def tn(a, b):
    return lax.dot_general(a, b, (((0,), (0,)), ((), ())), preferred_element_type=F32)


def mod(a, n):
    return lax.rem(a, jnp.int32(n))


def drain(ref, sem):
    pltpu.make_async_copy(ref, ref, sem).wait()


def remote(src, dst, ssem, rsem, dev):
    pltpu.make_async_remote_copy(
        src_ref=src, dst_ref=dst, send_sem=ssem, recv_sem=rsem, device_id=dev, device_id_type=MESH
    ).start()


def kernel(
    ids, gates, q, k, v, og, wg_h, wu_h, wd_h,
    qg_o, kg_o, vg_o, dwg_o, dwu_o, dwd_o,
    wg, wu, wd, sterm, srecv, sspan, stb, rtm, rt, xq, xg, pm, gs, sg, sh, yb, xb, mx, hid,
    act, gg, ug, part, rin, rout, rcin, rsin, red, rr, mg, stage,
    bterm, bz, bspan, bown, ball, qgs, qgb,
    wsem, st_s, st_r, sp_s, sp_r, sb_s, sb_r, xt_s, xt_r,
    sl_s, sl_r, mc_s, mc_l, mc_r, mc_f, rd_s, ri_r, rc_r, rs_r, rt_s, rt_r, stsem,
    bz_s, bz_r, bp_s, bp_r, bb_s, bb_r, qg_s, qg_r,
):
    tm = lax.axis_index("tm")
    e = lax.axis_index("expert")
    z = lax.div(e, jnp.int32(4))
    x = mod(e, 4)
    y = lax.div(tm, jnp.int32(2))
    c = mod(tm, 2)
    me = tm * 4 + z
    xr = mod(x + 1, 4)
    xl = mod(x + 3, 4)
    xf = mod(x + 2, 4)
    right = (tm, z * 4 + xr)
    left = (tm, z * 4 + xl)

    def cols(b):
        return pl.ds(pl.multiple_of(b * BC, BC), BC)

    bar = pltpu.get_barrier_semaphore()

    def greet_span(i, _):
        pl.semaphore_signal(bar, inc=1, device_id=(tm, mod(e + i, 16)), device_id_type=MESH)
        return 0

    lax.fori_loop(1, 16, greet_span, 0)

    def greet_plane(i, _):
        t = mod(tm + lax.div(i, jnp.int32(4)), 8)
        zz = mod(z + mod(i, 4), 4)
        pl.semaphore_signal(bar, inc=1, device_id=(t, zz * 4 + x), device_id_type=MESH)
        return 0

    lax.fori_loop(4, 32, greet_plane, 0)

    w_copies = []
    for i, (src, dst) in enumerate(((wg_h, wg), (wu_h, wu), (wd_h, wd))):
        cp = pltpu.make_async_copy(src.at[0], dst, wsem.at[i])
        cp.start()
        w_copies.append(cp)

    for h in range(16):
        sl = slice(h * HD, (h + 1) * HD)
        sterm[h] = tn(k[:, sl], v[:, sl]).astype(BF)

    eye = lax.broadcasted_iota(jnp.int32, (TOK, TOK), 0) == lax.broadcasted_iota(
        jnp.int32, (TOK, TOK), 1
    )
    upper = lax.broadcasted_iota(jnp.int32, (TOK, TOK), 0) < lax.broadcasted_iota(
        jnp.int32, (TOK, TOK), 1
    )
    upper = jnp.where(upper, 1.0, 0.0).astype(BF)
    idf = ids[...].astype(F32)
    gf = gates[...]

    def as_row(a, kk):
        return jnp.sum(jnp.where(eye, a[:, kk : kk + 1], 0.0), axis=0, keepdims=True)

    id_rows = [as_row(idf, kk) for kk in range(2)]
    lanes_e = lax.broadcasted_iota(jnp.int32, (NE, TOK), 0).astype(F32)
    hot = [jnp.where(lanes_e == r, 1.0, 0.0) for r in id_rows]
    earlier = nn((hot[0] + hot[1]).astype(BF), upper)
    rtm[...] = jnp.zeros_like(rtm)
    for kk in range(2):
        pos = jnp.sum(hot[kk] * earlier, axis=0, keepdims=True)
        rtm[kk : kk + 1, :] = jnp.where(pos < CAP, id_rows[kk] * G + pos, -4096.0)
        rtm[2 + kk : 3 + kk, :] = as_row(gf, kk)

    pl.semaphore_wait(bar, 43)

    def send_term(i, _):
        eo = mod(e + i, 16)
        ho = mod(eo, 4) * 4 + lax.div(eo, jnp.int32(4))
        remote(sterm.at[ho], srecv.at[e], st_s, st_r, (tm, eo))
        return 0

    lax.fori_loop(1, 16, send_term, 0)
    for i, (src, dst) in enumerate(((rtm, rt), (og, xg), (q, xq))):
        for d in range(1, 4):
            xo = mod(x + d, 4)
            s = src if i == 0 else src.at[:, cols(xo)]
            remote(s, dst.at[x], xt_s.at[i], xt_r.at[i], (tm, z * 4 + xo))
        s = src if i == 0 else src.at[:, cols(x)]
        pltpu.make_async_copy(s, dst.at[x], xt_r.at[i]).start()

    drain(srecv.at[pl.ds(0, 15)], st_r)
    srecv[e] = sterm[x * 4 + z]
    sspan[tm] = jnp.sum(srecv[...].astype(F32), axis=0)

    def send_span(i, _):
        remote(sspan.at[tm], sspan.at[tm], sp_s, sp_r, (mod(tm + i, 8), e))
        return 0

    lax.fori_loop(1, 8, send_span, 0)

    drain(rt, xt_r.at[0])

    def build(b, _):
        r0 = pl.multiple_of(b * 128, 128)
        ridx = (lax.broadcasted_iota(jnp.int32, (128, TOK), 0) + r0).astype(F32)
        acc = jnp.zeros((128, TOK), F32)
        for s in range(4):
            a = rt[s]
            m0 = ridx == a[0:1] + float(s * CAP)
            m1 = ridx == a[1:2] + float(s * CAP)
            pm[pl.ds(r0, 128), s * TOK : (s + 1) * TOK] = jnp.where(m0 | m1, 1.0, 0.0).astype(BF)
            acc = acc + jnp.where(m0, a[2:3], 0.0) + jnp.where(m1, a[3:4], 0.0)
        gs[pl.ds(r0, 128), :] = jnp.broadcast_to(jnp.sum(acc, axis=1, keepdims=True), (128, TOK))
        return 0

    lax.fori_loop(0, ROWS // 128, build, 0)

    def plane_rows(yy):
        return pl.ds(pl.multiple_of(yy * CH, CH), CH)

    def group_rows(g):
        return pl.ds(pl.multiple_of(g * G, G), G)

    def to_plane(src, dst, dcols, ssem, rsem, yy, self_too):
        def one(i, _):
            cc = mod(c + lax.div(i, jnp.int32(4)), 2)
            zz = mod(z + mod(i, 4), 4)
            t = yy * 2 + cc
            d = dst.at[group_rows(me)] if dcols is None else dst.at[group_rows(me), dcols]
            remote(src.at[group_rows(t * 4 + zz)], d, ssem, rsem, (t, zz * 4 + x))
            return 0

        lax.fori_loop(1 if self_too else 0, 8, one, 0)
        if self_too:
            d = dst.at[group_rows(me)] if dcols is None else dst.at[group_rows(me), dcols]
            pltpu.make_async_copy(src.at[group_rows(me)], d, rsem).start()

    def src_plane(j):
        return mod(y - DY[j] + 4, 4)

    def dst_plane(j):
        return mod(y + DY[j], 4)

    big = (yb, xb)
    small = (sg, sh)

    def wait_own(a, j):
        drain(big[a].at[plane_rows(src_plane(j)), cols(x)], sl_r.at[a, j])

    def cast(a, j):
        ref = big[a].at[plane_rows(src_plane(j)), cols(x)]
        remote(ref, ref, mc_s.at[a], mc_l.at[a, j], right)
        remote(ref, ref, mc_s.at[a], mc_r.at[a, j], left)

    def relay(a, j):
        rows = plane_rows(src_plane(j))
        from_left = big[a].at[rows, cols(xl)]
        from_right = big[a].at[rows, cols(xr)]
        drain(from_left, mc_l.at[a, j])
        if j % 2 == 0:
            remote(from_left, from_left, mc_s.at[a], mc_f.at[a, j], right)
        drain(from_right, mc_r.at[a, j])
        if j % 2 == 1:
            remote(from_right, from_right, mc_s.at[a], mc_f.at[a, j], left)

    def far(a, j):
        drain(big[a].at[plane_rows(src_plane(j)), cols(xf)], mc_f.at[a, j])

    drain(xg, xt_r.at[1])
    for j in range(4):
        rows = plane_rows(dst_plane(j))
        got = nn(pm[rows, :], xg[...].reshape(4 * TOK, BC))
        sg[rows, :] = (got * gs[rows, 0:1]).astype(BF)
        to_plane(sg, yb, cols(x), sl_s.at[0], sl_r.at[0, j], dst_plane(j), j == 0)

    drain(sspan.at[pl.ds(0, 7)], sp_r)
    total = jnp.zeros((HD, HD), F32)
    for t in range(8):
        total = total + jnp.where(t <= tm, sspan[t], 0.0)
    stb[z] = total.astype(BF)
    for d in range(1, 4):
        remote(stb.at[z], stb.at[z], sb_s, sb_r, (tm, mod(z + d, 4) * 4 + x))

    wait_own(0, 0)
    cast(0, 0)

    drain(xq, xt_r.at[2])
    drain(stb.at[pl.ds(0, 3)], sb_r)
    for i in range(4):
        sl = slice(i * HD, (i + 1) * HD)
        m = nn(xq[:, :, sl].reshape(4 * TOK, HD), stb[i])
        mx[:, sl] = m
        scale = lax.rsqrt(jnp.mean(m * m, axis=-1, keepdims=True) + EPS)
        hid[:, sl] = (m * scale).astype(BF)
    for j in range(4):
        rows = plane_rows(dst_plane(j))
        sh[rows, :] = nn(pm[rows, :], hid[...]).astype(BF)
        to_plane(sh, xb, cols(x), sl_s.at[1], sl_r.at[1, j], dst_plane(j), j == 0)

    for j in range(1, 4):
        wait_own(0, j)
        cast(0, j)
    for j in range(4):
        relay(0, j)
        wait_own(1, j)
        cast(1, j)

    for cp in w_copies:
        cp.wait()

    def compute(j):
        far(0, j)
        far(1, j)
        rows = plane_rows(src_plane(j))

        def hidden_cols(n, _):
            hc = pl.ds(pl.multiple_of(n * 256, 256), 256)
            gate = nn(xb[rows, :], wg[:, hc])
            up = nn(xb[rows, :], wu[:, hc])
            act_grad = nt(yb[rows, :], wd[hc, :])
            sigma = jax.nn.sigmoid(gate)
            silu = gate * sigma
            act[rows, hc] = (silu * up).astype(BF)
            gg[rows, hc] = (act_grad * up * sigma * (1.0 + gate * (1.0 - sigma))).astype(BF)
            ug[rows, hc] = (act_grad * silu).astype(BF)
            return 0

        lax.fori_loop(0, HID // 256, hidden_cols, 0)

        def part_cols(n, _):
            pc = cols(n)
            part[rows, pc] = (
                nt(gg[rows, :], wg[pc, :]) + nt(ug[rows, :], wu[pc, :])
            ).astype(BF)
            return 0

        lax.fori_loop(0, D // BC, part_cols, 0)
        if j % 2 == 0:
            remote(part.at[rows, cols(xf)], rin.at[j], rd_s, ri_r.at[j], right)
            remote(part.at[rows, cols(xl)], rsin.at[j], rd_s, rs_r.at[j], left)
        else:
            remote(part.at[rows, cols(xf)], rin.at[j], rd_s, ri_r.at[j], left)
            remote(part.at[rows, cols(xr)], rsin.at[j], rd_s, rs_r.at[j], right)

    def add_on(j):
        rows = plane_rows(src_plane(j))
        drain(rin.at[j], ri_r.at[j])
        near = xr if j % 2 == 0 else xl
        rout[j] = (rin[j].astype(F32) + part[rows, cols(near)].astype(F32)).astype(BF)
        remote(rout.at[j], rcin.at[j], rd_s, rc_r.at[j], right if j % 2 == 0 else left)

    def finish(j):
        yy = src_plane(j)
        rows = plane_rows(yy)
        drain(rsin.at[j], rs_r.at[j])
        drain(rcin.at[j], rc_r.at[j])
        red[rows, :] = (
            rcin[j].astype(F32) + rsin[j].astype(F32) + part[rows, cols(x)].astype(F32)
        ).astype(BF)
        to_plane(red, rr, None, rt_s, rt_r.at[j], yy, j == 0)

    def combine(j):
        rows = plane_rows(dst_plane(j))
        drain(rr.at[rows], rt_r.at[j])
        got = tn(pm[rows, :], rr[rows, :])
        if j == 0:
            mg[...] = got
        else:
            mg[...] += got

    def weights_in(s):
        slot = s % 2
        if s >= 2:
            for w, o in ((0, dwg_o), (1, dwu_o)):
                pltpu.make_async_copy(
                    stage.at[slot, w], o.at[0, (s - 2) * 512 : (s - 1) * 512, :], stsem.at[slot, w]
                ).wait()

        def one(n, _):
            r = pl.ds(pl.multiple_of(n * 256, 256), 256)
            xt = xb[:, pl.ds(pl.multiple_of(s * 512 + n * 256, 256), 256)]
            stage[slot, 0, r, :] = tn(xt, gg[...])
            stage[slot, 1, r, :] = tn(xt, ug[...])
            return 0

        lax.fori_loop(0, 2, one, 0)
        for w, o in ((0, dwg_o), (1, dwu_o)):
            pltpu.make_async_copy(
                stage.at[slot, w], o.at[0, s * 512 : (s + 1) * 512, :], stsem.at[slot, w]
            ).start()

    def weights_out(s):
        slot, w = divmod(s, 2)
        o = (dwg_o, dwu_o)[w]
        pltpu.make_async_copy(
            stage.at[slot, w], o.at[0, (2 + slot) * 512 : (3 + slot) * 512, :], stsem.at[slot, w]
        ).wait()

        def one(n, _):
            r = pl.ds(pl.multiple_of(n * 256, 256), 256)
            stage[slot, w, r, :] = tn(act[:, r], yb[:, s * 512 : (s + 1) * 512])
            return 0

        lax.fori_loop(0, 2, one, 0)
        pltpu.make_async_copy(
            stage.at[slot, w], dwd_o.at[0, :, s * 512 : (s + 1) * 512], stsem.at[slot, w]
        ).start()

    relay(1, 0)
    relay(1, 1)
    compute(0)
    relay(1, 2)
    compute(1)
    add_on(0)
    relay(1, 3)
    compute(2)
    add_on(1)
    compute(3)
    add_on(2)
    finish(0)
    weights_in(0)
    add_on(3)
    finish(1)
    weights_in(1)
    finish(2)
    weights_in(2)
    finish(3)
    weights_in(3)
    combine(0)
    weights_out(0)
    combine(1)
    weights_out(1)
    combine(2)
    weights_out(2)
    weights_out(3)
    combine(3)

    for i in range(4):
        sl = slice(i * HD, (i + 1) * HD)
        m = mx[:, sl]
        scale = lax.rsqrt(jnp.mean(m * m, axis=-1, keepdims=True) + EPS)
        normed = m * scale
        hg = xg[:, :, sl].reshape(4 * TOK, HD).astype(F32) + mg[:, sl]
        ng = scale * (hg - normed * jnp.mean(hg * normed, axis=-1, keepdims=True))
        ngb = ng.astype(BF)
        bterm[i] = tn(xq[:, :, sl].reshape(4 * TOK, HD), ngb).astype(BF)
        qgs[:, :, sl] = nt(ngb, stb[i]).astype(BF).reshape(4, TOK, HD)
    for d in range(1, 4):
        zo = mod(z + d, 4)
        remote(bterm.at[zo], bz.at[z], bz_s, bz_r, (tm, zo * 4 + x))
    for d in range(1, 4):
        xo = mod(x + d, 4)
        remote(qgs.at[xo], qgb.at[x], qg_s, qg_r, (tm, z * 4 + xo))
    drain(bz.at[pl.ds(0, 3)], bz_r)
    bz[z] = bterm[z]
    bspan[tm] = jnp.sum(bz[...].astype(F32), axis=0).astype(BF)

    def send_back_span(i, _):
        remote(bspan.at[tm], bspan.at[tm], bp_s, bp_r, (mod(tm + i, 8), e))
        return 0

    lax.fori_loop(1, 8, send_back_span, 0)
    drain(bspan.at[pl.ds(0, 7)], bp_r)
    total = jnp.zeros((HD, HD), F32)
    for t in range(8):
        total = total + jnp.where(t >= tm, bspan[t].astype(F32), 0.0)
    bown[...] = total.astype(BF)

    def send_back(i, _):
        remote(bown, ball.at[e], bb_s, bb_r, (tm, mod(e + i, 16)))
        return 0

    lax.fori_loop(1, 16, send_back, 0)
    drain(qgb.at[pl.ds(0, 3)], qg_r)
    qgb[x] = qgs[x]
    for b in range(4):
        qg_o[:, b * BC : (b + 1) * BC] = qgb[b]
    drain(ball.at[pl.ds(0, 15)], bb_r)
    ball[e] = bown[...]
    for eo in range(16):
        h = (eo % 4) * 4 + eo // 4
        sl = slice(h * HD, (h + 1) * HD)
        kg_o[:, sl] = nt(v[:, sl], ball[eo]).astype(BF)
        vg_o[:, sl] = nn(k[:, sl], ball[eo]).astype(BF)

    drain(sterm.at[pl.ds(0, 15)], st_s)
    drain(sspan.at[pl.ds(0, 7)], sp_s)
    drain(stb.at[pl.ds(0, 3)], sb_s)
    drain(rt.at[pl.ds(0, 3)], xt_s.at[0])
    drain(xg.at[pl.ds(0, 3)], xt_s.at[1])
    drain(xq.at[pl.ds(0, 3)], xt_s.at[2])
    for a in range(2):
        drain(small[a].at[pl.ds(0, 31 * G)], sl_s.at[a])
        for _ in range(3):
            drain(big[a].at[pl.ds(0, ROWS), pl.ds(0, BC)], mc_s.at[a])
    for _ in range(3):
        drain(red, rd_s)
    drain(red.at[pl.ds(0, 31 * G)], rt_s)
    drain(bz.at[pl.ds(0, 3)], bz_s)
    drain(bspan.at[pl.ds(0, 7)], bp_s)
    drain(ball.at[pl.ds(0, 15)], bb_s)
    drain(qgb.at[pl.ds(0, 3)], qg_s)
    for s in range(4):
        slot, w = divmod(s, 2)
        pltpu.make_async_copy(
            stage.at[slot, w], dwd_o.at[0, :, s * 512 : (s + 1) * 512], stsem.at[slot, w]
        ).wait()


def body(queries, keys, values, out_grad, expert_ids, combine_gates, gate_w, up_w, down_w):
    vm = pl.BlockSpec(memory_space=pltpu.VMEM)
    hbm = pl.BlockSpec(memory_space=pl.ANY)
    dma = pltpu.SemaphoreType.DMA
    scratch = [
        pltpu.VMEM((D, HID), BF),
        pltpu.VMEM((D, HID), BF),
        pltpu.VMEM((HID, D), BF),
        pltpu.VMEM((16, HD, HD), BF),
        pltpu.VMEM((16, HD, HD), BF),
        pltpu.VMEM((8, HD, HD), F32),
        pltpu.VMEM((4, HD, HD), BF),
        pltpu.VMEM((8, TOK), F32),
        pltpu.VMEM((4, 8, TOK), F32),
        pltpu.VMEM((4, TOK, BC), BF),
        pltpu.VMEM((4, TOK, BC), BF),
        pltpu.VMEM((ROWS, 4 * TOK), BF),
        pltpu.VMEM((ROWS, TOK), F32),
        pltpu.VMEM((ROWS, BC), BF),
        pltpu.VMEM((ROWS, BC), BF),
        pltpu.VMEM((ROWS, D), BF),
        pltpu.VMEM((ROWS, D), BF),
        pltpu.VMEM((4 * TOK, BC), F32),
        pltpu.VMEM((4 * TOK, BC), BF),
        pltpu.VMEM((ROWS, HID), BF),
        pltpu.VMEM((ROWS, HID), BF),
        pltpu.VMEM((ROWS, HID), BF),
        pltpu.VMEM((ROWS, D), BF),
        pltpu.VMEM((4, CH, BC), BF),
        pltpu.VMEM((4, CH, BC), BF),
        pltpu.VMEM((4, CH, BC), BF),
        pltpu.VMEM((4, CH, BC), BF),
        pltpu.VMEM((ROWS, BC), BF),
        pltpu.VMEM((ROWS, BC), BF),
        pltpu.VMEM((4 * TOK, BC), F32),
        pltpu.VMEM((2, 2, 512, 512), F32),
        pltpu.VMEM((4, HD, HD), BF),
        pltpu.VMEM((4, HD, HD), BF),
        pltpu.VMEM((8, HD, HD), BF),
        pltpu.VMEM((HD, HD), BF),
        pltpu.VMEM((16, HD, HD), BF),
        pltpu.VMEM((4, TOK, BC), BF),
        pltpu.VMEM((4, TOK, BC), BF),
        dma((3,)),
        dma, dma, dma, dma, dma, dma,
        dma((3,)), dma((3,)),
        dma((2,)), dma((2, 4)),
        dma((2,)), dma((2, 4)), dma((2, 4)), dma((2, 4)),
        dma, dma((4,)), dma((4,)), dma((4,)),
        dma, dma((4,)),
        dma((2, 2)),
        dma, dma, dma, dma, dma, dma, dma, dma,
    ]
    tokens = jax.ShapeDtypeStruct((TOK, D), BF)
    return pl.pallas_call(
        kernel,
        out_shape=(
            tokens,
            tokens,
            tokens,
            jax.ShapeDtypeStruct((1, D, HID), F32),
            jax.ShapeDtypeStruct((1, D, HID), F32),
            jax.ShapeDtypeStruct((1, HID, D), F32),
        ),
        in_specs=[vm] * 6 + [hbm] * 3,
        out_specs=(vm, vm, vm, hbm, hbm, hbm),
        scratch_shapes=scratch,
        compiler_params=pltpu.CompilerParams(
            collective_id=0, has_side_effects=True, vmem_limit_bytes=61 * 2**20
        ),
    )(expert_ids, combine_gates, queries, keys, values, out_grad, gate_w, up_w, down_w)


def solution(mesh):
    flat = P(("tm", "expert"), None)
    cube = P(("tm", "expert"), None, None)
    return jax.shard_map(
        body,
        mesh=mesh,
        in_specs=(flat,) * 6 + (cube,) * 3,
        out_specs=(flat,) * 3 + (cube,) * 3,
        check_vma=False,
    )
```

```python
import functools

import jax
import jax.numpy as jnp
from jax import lax
from jax.experimental import pallas as pl
from jax.experimental.pallas import tpu as pltpu
from jax.sharding import PartitionSpec as P

MESH = pl.DeviceIdType.MESH
EPS = 1e-06
TOK = 128
HD = 128
CAP = 12
G = 4 * CAP
NE = 32
ROWS = NE * G
CH = 8 * G
HF = CH // 2
BC = 512
D = 2048
HID = 512
DY = (0, 1, 3, 2)
STEPS = 4
BF = jnp.bfloat16
F32 = jnp.float32


def nn(a, b):
    return lax.dot_general(a, b, (((1,), (0,)), ((), ())), preferred_element_type=F32)


def nt(a, b):
    return lax.dot_general(a, b, (((1,), (1,)), ((), ())), preferred_element_type=F32)


def tn(a, b):
    return lax.dot_general(a, b, (((0,), (0,)), ((), ())), preferred_element_type=F32)


def mod(a, n):
    return lax.rem(a, jnp.int32(n))


def drain(ref, sem):
    pltpu.make_async_copy(ref, ref, sem).wait()


def remote(src, dst, ssem, rsem, dev):
    pltpu.make_async_remote_copy(
        src_ref=src, dst_ref=dst, send_sem=ssem, recv_sem=rsem, device_id=dev, device_id_type=MESH
    ).start()


def kernel(
    ids, gates, q, k_h, v_h, og, wg_h, wu_h, wd_h,
    qg_o, ball_o, dwg_o, dwu_o, dwd_o,
    k, v, wg, wu, wd, sterm, srecv, sspan, stb, rtm, rt, xq, xg, pm, gs, sg, sh, yb, xb, mx, hid,
    act, gg, ug, part, rin, rout, rcin, rsin, red, rr, mg, stage,
    bterm, bz, bspan, bown, ball, qgs, qgb,
    kvsem, wsem, st_s, st_r, sp_s, sp_r, sb_s, sb_r, xt_s, xt_r,
    sl_s, sl_r, mc_s, mc_l, mc_r, mc_f, rd_s, ri_r, rc_r, rs_r, rt_s, rt_r, stsem,
    bz_s, bz_r, bp_s, bp_r, bb_s, bb_r, qg_s, qg_r,
):
    tm = lax.axis_index("tm")
    e = lax.axis_index("expert")
    z = lax.div(e, jnp.int32(4))
    x = mod(e, 4)
    y = lax.div(tm, jnp.int32(2))
    c = mod(tm, 2)
    me = tm * 4 + z
    xr = mod(x + 1, 4)
    xl = mod(x + 3, 4)
    xf = mod(x + 2, 4)
    right = (tm, z * 4 + xr)
    left = (tm, z * 4 + xl)

    def cols(b):
        return pl.ds(pl.multiple_of(b * BC, BC), BC)

    bar = pltpu.get_barrier_semaphore()

    def greet_span(i, _):
        pl.semaphore_signal(bar, inc=1, device_id=(tm, mod(e + i, 16)), device_id_type=MESH)
        return 0

    lax.fori_loop(1, 16, greet_span, 0)

    def greet_plane(i, _):
        t = mod(tm + lax.div(i, jnp.int32(4)), 8)
        zz = mod(z + mod(i, 4), 4)
        pl.semaphore_signal(bar, inc=1, device_id=(t, zz * 4 + x), device_id_type=MESH)
        return 0

    lax.fori_loop(4, 32, greet_plane, 0)

    kv_copies = []
    for i, (src, dst) in enumerate(((k_h, k), (v_h, v))):
        cp = pltpu.make_async_copy(src, dst, kvsem.at[i])
        cp.start()
        kv_copies.append(cp)
    w_copies = []
    for i, (src, dst) in enumerate(((wg_h, wg), (wu_h, wu), (wd_h, wd))):
        cp = pltpu.make_async_copy(src.at[0], dst, wsem.at[i])
        cp.start()
        w_copies.append(cp)

    upper = lax.broadcasted_iota(jnp.int32, (TOK, TOK), 0) < lax.broadcasted_iota(
        jnp.int32, (TOK, TOK), 1
    )
    upper = jnp.where(upper, 1.0, 0.0).astype(BF)
    id_rows = [ids[kk : kk + 1, :].astype(F32) for kk in range(2)]
    lanes_e = lax.broadcasted_iota(jnp.int32, (NE, TOK), 0).astype(F32)
    hot = [jnp.where(lanes_e == r, 1.0, 0.0) for r in id_rows]
    earlier = nn((hot[0] + hot[1]).astype(BF), upper)
    rtm[...] = jnp.zeros_like(rtm)
    for kk in range(2):
        pos = jnp.sum(hot[kk] * earlier, axis=0, keepdims=True)
        rtm[kk : kk + 1, :] = jnp.where(pos < CAP, id_rows[kk] * G + pos, -4096.0)
        rtm[2 + kk : 3 + kk, :] = gates[kk : kk + 1, :]

    pl.semaphore_wait(bar, 43)

    def exchange(i, src, dst):
        for d in range(1, 4):
            xo = mod(x + d, 4)
            s = src if i == 0 else src.at[:, cols(xo)]
            remote(s, dst.at[x], xt_s.at[i], xt_r.at[i], (tm, z * 4 + xo))
        s = src if i == 0 else src.at[:, cols(x)]
        pltpu.make_async_copy(s, dst.at[x], xt_r.at[i]).start()

    exchange(0, rtm, rt)
    exchange(1, og, xg)

    for cp in kv_copies:
        cp.wait()
    for h in range(16):
        sl = slice(h * HD, (h + 1) * HD)
        sterm[h] = tn(k[:, sl], v[:, sl]).astype(BF)

    def send_term(i, _):
        eo = mod(e + i, 16)
        ho = mod(eo, 4) * 4 + lax.div(eo, jnp.int32(4))
        remote(sterm.at[ho], srecv.at[e], st_s, st_r, (tm, eo))
        return 0

    def build(r0):
        ridx = (lax.broadcasted_iota(jnp.int32, (128, TOK), 0) + r0).astype(F32)
        acc = jnp.zeros((128, TOK), F32)
        for s in range(4):
            a = rt[s]
            m0 = ridx == a[0:1] + float(s * CAP)
            m1 = ridx == a[1:2] + float(s * CAP)
            pm[pl.ds(r0, 128), s * TOK : (s + 1) * TOK] = jnp.where(m0 | m1, 1.0, 0.0).astype(BF)
            acc = acc + jnp.where(m0, a[2:3], 0.0) + jnp.where(m1, a[3:4], 0.0)
        gs[pl.ds(r0, 128), :] = jnp.broadcast_to(jnp.sum(acc, axis=1, keepdims=True), (128, TOK))

    def plane_rows(yy):
        return pl.ds(pl.multiple_of(yy * CH, CH), CH)

    def group_rows(g):
        return pl.ds(pl.multiple_of(g * G, G), G)

    def to_plane(src, dst, dcols, ssem, rsem, yy, self_too):
        def one(i, _):
            cc = mod(c + lax.div(i, jnp.int32(4)), 2)
            zz = mod(z + mod(i, 4), 4)
            t = yy * 2 + cc
            d = dst.at[group_rows(me)] if dcols is None else dst.at[group_rows(me), dcols]
            remote(src.at[group_rows(t * 4 + zz)], d, ssem, rsem, (t, zz * 4 + x))
            return 0

        lax.fori_loop(1 if self_too else 0, 8, one, 0)
        if self_too:
            d = dst.at[group_rows(me)] if dcols is None else dst.at[group_rows(me), dcols]
            pltpu.make_async_copy(src.at[group_rows(me)], d, rsem).start()

    def src_plane(j):
        return mod(y - DY[j] + 4, 4)

    def dst_plane(j):
        return mod(y + DY[j], 4)

    big = (yb, xb)
    small = (sg, sh)

    def wait_own(a, j):
        drain(big[a].at[plane_rows(src_plane(j)), cols(x)], sl_r.at[a, j])

    def cast(a, j):
        ref = big[a].at[plane_rows(src_plane(j)), cols(x)]
        remote(ref, ref, mc_s.at[a], mc_l.at[a, j], right)
        remote(ref, ref, mc_s.at[a], mc_r.at[a, j], left)

    def halves(j):
        start = src_plane(j) * CH
        return [pl.ds(pl.multiple_of(start + i * HF, HF), HF) for i in range(2)]

    def relay(a, j):
        rows = plane_rows(src_plane(j))
        upper_half, lower_half = halves(j)
        drain(big[a].at[rows, cols(xl)], mc_l.at[a, j])
        ref = big[a].at[upper_half, cols(xl)]
        remote(ref, ref, mc_s.at[a], mc_f.at[a, j], right)
        drain(big[a].at[rows, cols(xr)], mc_r.at[a, j])
        ref = big[a].at[lower_half, cols(xr)]
        remote(ref, ref, mc_s.at[a], mc_f.at[a, j], left)

    def far(a, j):
        drain(big[a].at[plane_rows(src_plane(j)), cols(xf)], mc_f.at[a, j])

    drain(rt, xt_r.at[0])

    def build_all(b, _):
        build(pl.multiple_of(b * 128, 128))
        return 0

    lax.fori_loop(0, ROWS // 128, build_all, 0)
    drain(xg, xt_r.at[1])
    lax.fori_loop(1, 16, send_term, 0)
    exchange(2, q, xq)
    for j in range(4):
        rows = plane_rows(dst_plane(j))
        got = nn(pm[rows, :], xg[...].reshape(4 * TOK, BC))
        sg[rows, :] = (got * gs[rows, 0:1]).astype(BF)
        to_plane(sg, yb, cols(x), sl_s.at[0], sl_r.at[0, j], dst_plane(j), j == 0)

    for j in range(2):
        wait_own(0, j)
        cast(0, j)
    drain(srecv.at[pl.ds(0, 15)], st_r)
    srecv[e] = sterm[x * 4 + z]
    sspan[tm] = jnp.sum(srecv[...].astype(F32), axis=0).astype(BF)

    def send_span(i, _):
        remote(sspan.at[tm], sspan.at[tm], sp_s, sp_r, (mod(tm + i, 8), e))
        return 0

    lax.fori_loop(1, 8, send_span, 0)
    for j in range(2, 4):
        wait_own(0, j)
        cast(0, j)

    drain(sspan.at[pl.ds(0, 7)], sp_r)
    total = jnp.zeros((HD, HD), F32)
    for t in range(8):
        total = total + jnp.where(t <= tm, sspan[t].astype(F32), 0.0)
    stb[z] = total.astype(BF)
    for d in range(1, 4):
        remote(stb.at[z], stb.at[z], sb_s, sb_r, (tm, mod(z + d, 4) * 4 + x))
    drain(stb.at[pl.ds(0, 3)], sb_r)
    drain(xq, xt_r.at[2])
    for i in range(4):
        sl = slice(i * HD, (i + 1) * HD)
        m = nn(xq[:, :, sl].reshape(4 * TOK, HD), stb[i])
        mx[:, sl] = m
        scale = lax.rsqrt(jnp.mean(m * m, axis=-1, keepdims=True) + EPS)
        hid[:, sl] = (m * scale).astype(BF)
    for j in range(4):
        rows = plane_rows(dst_plane(j))
        sh[rows, :] = nn(pm[rows, :], hid[...]).astype(BF)
        to_plane(sh, xb, cols(x), sl_s.at[1], sl_r.at[1, j], dst_plane(j), j == 0)

    for j in range(4):
        relay(0, j)
        wait_own(1, j)
        cast(1, j)

    for cp in w_copies:
        cp.wait()

    def compute(j):
        far(0, j)
        far(1, j)
        rows = plane_rows(src_plane(j))

        def hidden_cols(n, _):
            hc = pl.ds(pl.multiple_of(n * 256, 256), 256)
            gate = nn(xb[rows, :], wg[:, hc])
            up = nn(xb[rows, :], wu[:, hc])
            act_grad = nt(yb[rows, :], wd[hc, :])
            sigma = jax.nn.sigmoid(gate)
            silu = gate * sigma
            act[rows, hc] = (silu * up).astype(BF)
            gg[rows, hc] = (act_grad * up * sigma * (1.0 + gate * (1.0 - sigma))).astype(BF)
            ug[rows, hc] = (act_grad * silu).astype(BF)
            return 0

        lax.fori_loop(0, HID // 256, hidden_cols, 0)

        def part_cols(n, _):
            pc = cols(n)
            part[rows, pc] = (
                nt(gg[rows, :], wg[pc, :]) + nt(ug[rows, :], wu[pc, :])
            ).astype(BF)
            return 0

        lax.fori_loop(0, D // BC, part_cols, 0)
        up_h, low_h = halves(j)
        top, low = pl.ds(0, HF), pl.ds(HF, HF)
        remote(part.at[up_h, cols(xf)], rin.at[j, top], rd_s, ri_r.at[j], right)
        remote(part.at[low_h, cols(xf)], rin.at[j, low], rd_s, ri_r.at[j], left)
        remote(part.at[up_h, cols(xl)], rsin.at[j, top], rd_s, rs_r.at[j], left)
        remote(part.at[low_h, cols(xr)], rsin.at[j, low], rd_s, rs_r.at[j], right)

    def add_on(j):
        up_h, low_h = halves(j)
        drain(rin.at[j], ri_r.at[j])
        for h, rows, near, dev in ((0, up_h, xr, right), (1, low_h, xl, left)):
            sl = slice(h * HF, (h + 1) * HF)
            rout[j, sl] = (rin[j, sl].astype(F32) + part[rows, cols(near)].astype(F32)).astype(BF)
            half = pl.ds(h * HF, HF)
            remote(rout.at[j, half], rcin.at[j, half], rd_s, rc_r.at[j], dev)

    def finish(j):
        yy = src_plane(j)
        rows = plane_rows(yy)
        drain(rsin.at[j], rs_r.at[j])
        drain(rcin.at[j], rc_r.at[j])
        red[rows, :] = (
            rcin[j].astype(F32) + rsin[j].astype(F32) + part[rows, cols(x)].astype(F32)
        ).astype(BF)
        to_plane(red, rr, None, rt_s, rt_r.at[j], yy, j == 0)

    def combine(j):
        rows = plane_rows(dst_plane(j))
        drain(rr.at[rows], rt_r.at[j])
        got = tn(pm[rows, :], rr[rows, :])
        if j == 0:
            mg[...] = got
        else:
            mg[...] += got

    def weights_in(s):
        slot = s % 2
        if s >= 2:
            for w, o in ((0, dwg_o), (1, dwu_o)):
                pltpu.make_async_copy(
                    stage.at[slot, w], o.at[0, (s - 2) * 512 : (s - 1) * 512, :], stsem.at[slot, w]
                ).wait()

        def one(n, _):
            r = pl.ds(pl.multiple_of(n * 256, 256), 256)
            xt = xb[:, pl.ds(pl.multiple_of(s * 512 + n * 256, 256), 256)]
            stage[slot, 0, r, :] = tn(xt, gg[...])
            stage[slot, 1, r, :] = tn(xt, ug[...])
            return 0

        lax.fori_loop(0, 2, one, 0)
        for w, o in ((0, dwg_o), (1, dwu_o)):
            pltpu.make_async_copy(
                stage.at[slot, w], o.at[0, s * 512 : (s + 1) * 512, :], stsem.at[slot, w]
            ).start()

    def weights_out(s):
        slot, w = divmod(s, 2)
        o = (dwg_o, dwu_o)[w]
        pltpu.make_async_copy(
            stage.at[slot, w], o.at[0, (2 + slot) * 512 : (3 + slot) * 512, :], stsem.at[slot, w]
        ).wait()

        def one(n, _):
            r = pl.ds(pl.multiple_of(n * 256, 256), 256)
            stage[slot, w, r, :] = tn(act[:, r], yb[:, s * 512 : (s + 1) * 512])
            return 0

        lax.fori_loop(0, 2, one, 0)
        pltpu.make_async_copy(
            stage.at[slot, w], dwd_o.at[0, :, s * 512 : (s + 1) * 512], stsem.at[slot, w]
        ).start()

    relay(1, 0)
    relay(1, 1)
    relay(1, 2)
    compute(0)
    relay(1, 3)
    compute(1)
    compute(2)
    add_on(0)
    compute(3)
    add_on(1)
    add_on(2)
    add_on(3)
    finish(0)
    finish(1)
    weights_in(0)
    weights_in(1)
    finish(2)
    weights_in(2)
    weights_in(3)
    combine(0)
    finish(3)
    combine(1)
    combine(2)
    weights_out(0)
    combine(3)

    for i in range(4):
        sl = slice(i * HD, (i + 1) * HD)
        m = mx[:, sl]
        scale = lax.rsqrt(jnp.mean(m * m, axis=-1, keepdims=True) + EPS)
        normed = m * scale
        hg = xg[:, :, sl].reshape(4 * TOK, HD).astype(F32) + mg[:, sl]
        ng = scale * (hg - normed * jnp.mean(hg * normed, axis=-1, keepdims=True))
        ngb = ng.astype(BF)
        bterm[i] = tn(xq[:, :, sl].reshape(4 * TOK, HD), ngb).astype(BF)
        qgs[:, :, sl] = nt(ngb, stb[i]).astype(BF).reshape(4, TOK, HD)
    for d in range(1, 4):
        zo = mod(z + d, 4)
        remote(bterm.at[zo], bz.at[z], bz_s, bz_r, (tm, zo * 4 + x))
    for d in range(1, 4):
        xo = mod(x + d, 4)
        remote(qgs.at[xo], qgb.at[x], qg_s, qg_r, (tm, z * 4 + xo))
    weights_out(1)
    drain(bz.at[pl.ds(0, 3)], bz_r)
    bz[z] = bterm[z]
    bspan[tm] = jnp.sum(bz[...].astype(F32), axis=0).astype(BF)

    def send_back_span(i, _):
        remote(bspan.at[tm], bspan.at[tm], bp_s, bp_r, (mod(tm + i, 8), e))
        return 0

    lax.fori_loop(1, 8, send_back_span, 0)
    weights_out(2)
    drain(bspan.at[pl.ds(0, 7)], bp_r)
    total = jnp.zeros((HD, HD), F32)
    for t in range(8):
        total = total + jnp.where(t >= tm, bspan[t].astype(F32), 0.0)
    bown[...] = total.astype(BF)

    def send_back(i, _):
        remote(bown, ball.at[e], bb_s, bb_r, (tm, mod(e + i, 16)))
        return 0

    lax.fori_loop(1, 16, send_back, 0)
    weights_out(3)
    drain(qgb.at[pl.ds(0, 3)], qg_r)
    qgb[x] = qgs[x]
    for b in range(4):
        qg_o[:, b * BC : (b + 1) * BC] = qgb[b]
    drain(ball.at[pl.ds(0, 15)], bb_r)
    ball[e] = bown[...]
    for eo in range(16):
        ball_o[(eo % 4) * 4 + eo // 4] = ball[eo]

    drain(sterm.at[pl.ds(0, 15)], st_s)
    drain(sspan.at[pl.ds(0, 7)], sp_s)
    drain(stb.at[pl.ds(0, 3)], sb_s)
    drain(rt.at[pl.ds(0, 3)], xt_s.at[0])
    drain(xg.at[pl.ds(0, 3)], xt_s.at[1])
    drain(xq.at[pl.ds(0, 3)], xt_s.at[2])
    for a in range(2):
        drain(small[a].at[pl.ds(0, 31 * G)], sl_s.at[a])
        for _ in range(3):
            drain(big[a].at[pl.ds(0, ROWS), pl.ds(0, BC)], mc_s.at[a])
    for _ in range(3):
        drain(red, rd_s)
    drain(red.at[pl.ds(0, 31 * G)], rt_s)
    drain(bz.at[pl.ds(0, 3)], bz_s)
    drain(bspan.at[pl.ds(0, 7)], bp_s)
    drain(ball.at[pl.ds(0, 15)], bb_s)
    drain(qgb.at[pl.ds(0, 3)], qg_s)
    for s in range(4):
        slot, w = divmod(s, 2)
        pltpu.make_async_copy(
            stage.at[slot, w], dwd_o.at[0, :, s * 512 : (s + 1) * 512], stsem.at[slot, w]
        ).wait()


def finish_kernel(qg, ball, k, v, dwg, dwu, dwd, qg_o, kg_o, vg_o, dwg_o, dwu_o, dwd_o):
    qg_o[...] = qg[...]
    dwg_o[...] = dwg[...]
    dwu_o[...] = dwu[...]
    dwd_o[...] = dwd[...]
    for i in range(16 // STEPS):
        sl = slice(i * HD, (i + 1) * HD)
        kg_o[:, sl] = nt(v[:, sl], ball[i]).astype(BF)
        vg_o[:, sl] = nn(k[:, sl], ball[i]).astype(BF)


def body(queries, keys, values, out_grad, expert_ids, combine_gates, gate_w, up_w, down_w):
    vm = pl.BlockSpec(memory_space=pltpu.VMEM)
    hbm = pl.BlockSpec(memory_space=pl.ANY)
    dma = pltpu.SemaphoreType.DMA
    scratch = [
        pltpu.VMEM((TOK, D), BF),
        pltpu.VMEM((TOK, D), BF),
        pltpu.VMEM((D, HID), BF),
        pltpu.VMEM((D, HID), BF),
        pltpu.VMEM((HID, D), BF),
        pltpu.VMEM((16, HD, HD), BF),
        pltpu.VMEM((16, HD, HD), BF),
        pltpu.VMEM((8, HD, HD), BF),
        pltpu.VMEM((4, HD, HD), BF),
        pltpu.VMEM((8, TOK), F32),
        pltpu.VMEM((4, 8, TOK), F32),
        pltpu.VMEM((4, TOK, BC), BF),
        pltpu.VMEM((4, TOK, BC), BF),
        pltpu.VMEM((ROWS, 4 * TOK), BF),
        pltpu.VMEM((ROWS, TOK), F32),
        pltpu.VMEM((ROWS, BC), BF),
        pltpu.VMEM((ROWS, BC), BF),
        pltpu.VMEM((ROWS, D), BF),
        pltpu.VMEM((ROWS, D), BF),
        pltpu.VMEM((4 * TOK, BC), F32),
        pltpu.VMEM((4 * TOK, BC), BF),
        pltpu.VMEM((ROWS, HID), BF),
        pltpu.VMEM((ROWS, HID), BF),
        pltpu.VMEM((ROWS, HID), BF),
        pltpu.VMEM((ROWS, D), BF),
        pltpu.VMEM((4, CH, BC), BF),
        pltpu.VMEM((4, CH, BC), BF),
        pltpu.VMEM((4, CH, BC), BF),
        pltpu.VMEM((4, CH, BC), BF),
        pltpu.VMEM((ROWS, BC), BF),
        pltpu.VMEM((ROWS, BC), BF),
        pltpu.VMEM((4 * TOK, BC), F32),
        pltpu.VMEM((2, 2, 512, 512), F32),
        pltpu.VMEM((4, HD, HD), BF),
        pltpu.VMEM((4, HD, HD), BF),
        pltpu.VMEM((8, HD, HD), BF),
        pltpu.VMEM((HD, HD), BF),
        pltpu.VMEM((16, HD, HD), BF),
        pltpu.VMEM((4, TOK, BC), BF),
        pltpu.VMEM((4, TOK, BC), BF),
        dma((2,)),
        dma((3,)),
        dma, dma, dma, dma, dma, dma,
        dma((3,)), dma((3,)),
        dma((2,)), dma((2, 4)),
        dma((2,)), dma((2, 4)), dma((2, 4)), dma((2, 4)),
        dma, dma((4,)), dma((4,)), dma((4,)),
        dma, dma((4,)),
        dma((2, 2)),
        dma, dma, dma, dma, dma, dma, dma, dma,
    ]
    tokens = jax.ShapeDtypeStruct((TOK, D), BF)
    grads_in = jax.ShapeDtypeStruct((1, D, HID), F32)
    grads_out = jax.ShapeDtypeStruct((1, HID, D), F32)
    query_grad, back, gate_g, up_g, down_g = pl.pallas_call(
        kernel,
        out_shape=(
            tokens,
            jax.ShapeDtypeStruct((16, HD, HD), BF),
            grads_in,
            grads_in,
            grads_out,
        ),
        in_specs=[vm] * 2 + [hbm] * 7,
        out_specs=(vm, vm, hbm, hbm, hbm),
        scratch_shapes=scratch,
        compiler_params=pltpu.CompilerParams(
            collective_id=0, has_side_effects=True, vmem_limit_bytes=61 * 2**20
        ),
    )(expert_ids.T, combine_gates.T, queries, keys, values, out_grad, gate_w, up_w, down_w)
    lanes = pl.BlockSpec((TOK, D // STEPS), lambda i: (0, i))
    wide = pl.BlockSpec((1, D // STEPS, HID), lambda i: (0, i, 0))
    tall = pl.BlockSpec((1, HID // STEPS, D), lambda i: (0, i, 0))
    return pl.pallas_call(
        finish_kernel,
        out_shape=(tokens, tokens, tokens, grads_in, grads_in, grads_out),
        grid=(STEPS,),
        in_specs=[lanes, pl.BlockSpec((16 // STEPS, HD, HD), lambda i: (i, 0, 0)), lanes, lanes, wide, wide, tall],
        out_specs=(lanes, lanes, lanes, wide, wide, tall),
    )(query_grad, back, keys, values, gate_g, up_g, down_g)


def solution(mesh):
    flat = P(("tm", "expert"), None)
    cube = P(("tm", "expert"), None, None)
    return jax.shard_map(
        body,
        mesh=mesh,
        in_specs=(flat,) * 6 + (cube,) * 3,
        out_specs=(flat,) * 3 + (cube,) * 3,
        check_vma=False,
    )
```

```python
import functools

import jax
import jax.numpy as jnp
from jax import lax
from jax.experimental import pallas as pl
from jax.experimental.pallas import tpu as pltpu
from jax.sharding import PartitionSpec as P

MESH = pl.DeviceIdType.MESH
EPS = 1e-06
TOK = 128
HD = 128
CAP = 12
G = 4 * CAP
NE = 32
ROWS = NE * G
CH = 8 * G
HF = CH // 2
BC = 512
D = 2048
HID = 512
DY = (0, 1, 3, 2)
STEPS = 4
BF = jnp.bfloat16
F32 = jnp.float32


def nn(a, b):
    return lax.dot_general(a, b, (((1,), (0,)), ((), ())), preferred_element_type=F32)


def nt(a, b):
    return lax.dot_general(a, b, (((1,), (1,)), ((), ())), preferred_element_type=F32)


def tn(a, b):
    return lax.dot_general(a, b, (((0,), (0,)), ((), ())), preferred_element_type=F32)


def mod(a, n):
    return lax.rem(a, jnp.int32(n))


def drain(ref, sem):
    pltpu.make_async_copy(ref, ref, sem).wait()


def remote(src, dst, ssem, rsem, dev):
    pltpu.make_async_remote_copy(
        src_ref=src, dst_ref=dst, send_sem=ssem, recv_sem=rsem, device_id=dev, device_id_type=MESH
    ).start()


def kernel(
    ids, gates, q, k_h, v_h, og, wg_h, wu_h, wd_h,
    qg_o, ball_o, dwg_o, dwu_o, dwd_o,
    k, v, wg, wu, wd, sterm, srecv, szsum, sxrecv, sspan, stb, rtm, rt, xq, xg, pm, gs, sg, sh, yb, xb, mx, hid,
    act, gg, ug, part, rin, rout, rcin, rsin, red, rr, mg, stage,
    bterm, bz, bspan, bown, ball, qgs, qgb,
    kvsem, wsem, st_s, st_r, sx_s, sx_r, sp_s, sp_r, sb_s, sb_r, xt_s, xt_r,
    sl_s, sl_r, mc_s, mc_l, mc_r, mc_f, rd_s, ri_r, rc_r, rs_r, rt_s, rt_r, stsem,
    bz_s, bz_r, bp_s, bp_r, bb_s, bb_r, qg_s, qg_r,
):
    tm = lax.axis_index("tm")
    e = lax.axis_index("expert")
    z = lax.div(e, jnp.int32(4))
    x = mod(e, 4)
    y = lax.div(tm, jnp.int32(2))
    c = mod(tm, 2)
    me = tm * 4 + z
    xr = mod(x + 1, 4)
    xl = mod(x + 3, 4)
    xf = mod(x + 2, 4)
    right = (tm, z * 4 + xr)
    left = (tm, z * 4 + xl)

    def cols(b):
        return pl.ds(pl.multiple_of(b * BC, BC), BC)

    bar = pltpu.get_barrier_semaphore()

    def greet_span(i, _):
        pl.semaphore_signal(bar, inc=1, device_id=(tm, mod(e + i, 16)), device_id_type=MESH)
        return 0

    lax.fori_loop(1, 16, greet_span, 0)

    def greet_plane(i, _):
        t = mod(tm + lax.div(i, jnp.int32(4)), 8)
        zz = mod(z + mod(i, 4), 4)
        pl.semaphore_signal(bar, inc=1, device_id=(t, zz * 4 + x), device_id_type=MESH)
        return 0

    lax.fori_loop(4, 32, greet_plane, 0)

    kv_copies = []
    for i, (src, dst) in enumerate(((k_h, k), (v_h, v))):
        cp = pltpu.make_async_copy(src, dst, kvsem.at[i])
        cp.start()
        kv_copies.append(cp)
    w_copies = []
    for i, (src, dst) in enumerate(((wg_h, wg), (wu_h, wu), (wd_h, wd))):
        cp = pltpu.make_async_copy(src.at[0], dst, wsem.at[i])
        cp.start()
        w_copies.append(cp)

    upper = lax.broadcasted_iota(jnp.int32, (TOK, TOK), 0) < lax.broadcasted_iota(
        jnp.int32, (TOK, TOK), 1
    )
    upper = jnp.where(upper, 1.0, 0.0).astype(BF)
    id_rows = [ids[kk : kk + 1, :].astype(F32) for kk in range(2)]
    lanes_e = lax.broadcasted_iota(jnp.int32, (NE, TOK), 0).astype(F32)
    hot = [jnp.where(lanes_e == r, 1.0, 0.0) for r in id_rows]
    earlier = nn((hot[0] + hot[1]).astype(BF), upper)
    rtm[...] = jnp.zeros_like(rtm)
    for kk in range(2):
        pos = jnp.sum(hot[kk] * earlier, axis=0, keepdims=True)
        rtm[kk : kk + 1, :] = jnp.where(pos < CAP, id_rows[kk] * G + pos, -4096.0)
        rtm[2 + kk : 3 + kk, :] = gates[kk : kk + 1, :]

    pl.semaphore_wait(bar, 43)

    def exchange(i, src, dst):
        for d in range(1, 4):
            xo = mod(x + d, 4)
            s = src if i == 0 else src.at[:, cols(xo)]
            remote(s, dst.at[x], xt_s.at[i], xt_r.at[i], (tm, z * 4 + xo))
        s = src if i == 0 else src.at[:, cols(x)]
        pltpu.make_async_copy(s, dst.at[x], xt_r.at[i]).start()

    exchange(0, rtm, rt)
    exchange(1, og, xg)

    for cp in kv_copies:
        cp.wait()
    for h in range(16):
        sl = slice(h * HD, (h + 1) * HD)
        sterm[h % 4, h // 4] = tn(k[:, sl], v[:, sl]).astype(BF)

    for d in range(1, 4):
        zo = mod(z + d, 4)
        remote(sterm.at[zo], srecv.at[z], st_s, st_r, (tm, zo * 4 + x))

    def build(r0):
        ridx = (lax.broadcasted_iota(jnp.int32, (128, TOK), 0) + r0).astype(F32)
        acc = jnp.zeros((128, TOK), F32)
        for s in range(4):
            a = rt[s]
            m0 = ridx == a[0:1] + float(s * CAP)
            m1 = ridx == a[1:2] + float(s * CAP)
            pm[pl.ds(r0, 128), s * TOK : (s + 1) * TOK] = jnp.where(m0 | m1, 1.0, 0.0).astype(BF)
            acc = acc + jnp.where(m0, a[2:3], 0.0) + jnp.where(m1, a[3:4], 0.0)
        gs[pl.ds(r0, 128), :] = jnp.broadcast_to(jnp.sum(acc, axis=1, keepdims=True), (128, TOK))

    def plane_rows(yy):
        return pl.ds(pl.multiple_of(yy * CH, CH), CH)

    def group_rows(g):
        return pl.ds(pl.multiple_of(g * G, G), G)

    def to_plane(src, dst, dcols, ssem, rsem, yy, self_too):
        def one(i, _):
            cc = mod(c + lax.div(i, jnp.int32(4)), 2)
            zz = mod(z + mod(i, 4), 4)
            t = yy * 2 + cc
            d = dst.at[group_rows(me)] if dcols is None else dst.at[group_rows(me), dcols]
            remote(src.at[group_rows(t * 4 + zz)], d, ssem, rsem, (t, zz * 4 + x))
            return 0

        lax.fori_loop(1 if self_too else 0, 8, one, 0)
        if self_too:
            d = dst.at[group_rows(me)] if dcols is None else dst.at[group_rows(me), dcols]
            pltpu.make_async_copy(src.at[group_rows(me)], d, rsem).start()

    def src_plane(j):
        return mod(y - DY[j] + 4, 4)

    def dst_plane(j):
        return mod(y + DY[j], 4)

    big = (yb, xb)
    small = (sg, sh)

    def wait_own(a, j):
        drain(big[a].at[plane_rows(src_plane(j)), cols(x)], sl_r.at[a, j])

    def cast(a, j):
        ref = big[a].at[plane_rows(src_plane(j)), cols(x)]
        remote(ref, ref, mc_s.at[a], mc_l.at[a, j], right)
        remote(ref, ref, mc_s.at[a], mc_r.at[a, j], left)

    def halves(j):
        start = src_plane(j) * CH
        return [pl.ds(pl.multiple_of(start + i * HF, HF), HF) for i in range(2)]

    def relay(a, j):
        rows = plane_rows(src_plane(j))
        upper_half, lower_half = halves(j)
        drain(big[a].at[rows, cols(xl)], mc_l.at[a, j])
        ref = big[a].at[upper_half, cols(xl)]
        remote(ref, ref, mc_s.at[a], mc_f.at[a, j], right)
        drain(big[a].at[rows, cols(xr)], mc_r.at[a, j])
        ref = big[a].at[lower_half, cols(xr)]
        remote(ref, ref, mc_s.at[a], mc_f.at[a, j], left)

    def far(a, j):
        drain(big[a].at[plane_rows(src_plane(j)), cols(xf)], mc_f.at[a, j])

    drain(rt, xt_r.at[0])

    def build_all(b, _):
        build(pl.multiple_of(b * 128, 128))
        return 0

    lax.fori_loop(0, ROWS // 128, build_all, 0)
    drain(xg, xt_r.at[1])
    drain(srecv.at[pl.ds(0, 3)], st_r)
    srecv[z] = sterm[z]
    szsum[...] = jnp.sum(srecv[...].astype(F32), axis=0).astype(BF)
    for d in range(1, 4):
        xo = mod(x + d, 4)
        remote(szsum.at[xo], sxrecv.at[x], sx_s, sx_r, (tm, z * 4 + xo))
    exchange(2, q, xq)
    for j in range(4):
        rows = plane_rows(dst_plane(j))
        got = nn(pm[rows, :], xg[...].reshape(4 * TOK, BC))
        sg[rows, :] = (got * gs[rows, 0:1]).astype(BF)
        to_plane(sg, yb, cols(x), sl_s.at[0], sl_r.at[0, j], dst_plane(j), j == 0)

    for j in range(2):
        wait_own(0, j)
        cast(0, j)
    drain(sxrecv.at[pl.ds(0, 3)], sx_r)
    sxrecv[x] = szsum[x]
    sspan[tm] = jnp.sum(sxrecv[...].astype(F32), axis=0).astype(BF)

    def send_span(i, _):
        remote(sspan.at[tm], sspan.at[tm], sp_s, sp_r, (mod(tm + i, 8), e))
        return 0

    lax.fori_loop(1, 8, send_span, 0)
    for j in range(2, 4):
        wait_own(0, j)
        cast(0, j)

    drain(sspan.at[pl.ds(0, 7)], sp_r)
    total = jnp.zeros((HD, HD), F32)
    for t in range(8):
        total = total + jnp.where(t <= tm, sspan[t].astype(F32), 0.0)
    stb[z] = total.astype(BF)
    for d in range(1, 4):
        remote(stb.at[z], stb.at[z], sb_s, sb_r, (tm, mod(z + d, 4) * 4 + x))
    drain(stb.at[pl.ds(0, 3)], sb_r)
    drain(xq, xt_r.at[2])
    for i in range(4):
        sl = slice(i * HD, (i + 1) * HD)
        m = nn(xq[:, :, sl].reshape(4 * TOK, HD), stb[i])
        mx[:, sl] = m
        scale = lax.rsqrt(jnp.mean(m * m, axis=-1, keepdims=True) + EPS)
        hid[:, sl] = (m * scale).astype(BF)
    for j in range(4):
        rows = plane_rows(dst_plane(j))
        sh[rows, :] = nn(pm[rows, :], hid[...]).astype(BF)
        to_plane(sh, xb, cols(x), sl_s.at[1], sl_r.at[1, j], dst_plane(j), j == 0)

    for j in range(4):
        relay(0, j)
        wait_own(1, j)
        cast(1, j)

    for cp in w_copies:
        cp.wait()

    def compute(j):
        far(0, j)
        far(1, j)
        rows = plane_rows(src_plane(j))

        def hidden_cols(n, _):
            hc = pl.ds(pl.multiple_of(n * 256, 256), 256)
            gate = nn(xb[rows, :], wg[:, hc])
            up = nn(xb[rows, :], wu[:, hc])
            act_grad = nt(yb[rows, :], wd[hc, :])
            sigma = jax.nn.sigmoid(gate)
            silu = gate * sigma
            act[rows, hc] = (silu * up).astype(BF)
            gg[rows, hc] = (act_grad * up * sigma * (1.0 + gate * (1.0 - sigma))).astype(BF)
            ug[rows, hc] = (act_grad * silu).astype(BF)
            return 0

        lax.fori_loop(0, HID // 256, hidden_cols, 0)

        def part_cols(n, _):
            pc = cols(n)
            part[rows, pc] = (
                nt(gg[rows, :], wg[pc, :]) + nt(ug[rows, :], wu[pc, :])
            ).astype(BF)
            return 0

        lax.fori_loop(0, D // BC, part_cols, 0)
        up_h, low_h = halves(j)
        top, low = pl.ds(0, HF), pl.ds(HF, HF)
        remote(part.at[up_h, cols(xf)], rin.at[j, top], rd_s, ri_r.at[j], right)
        remote(part.at[low_h, cols(xf)], rin.at[j, low], rd_s, ri_r.at[j], left)
        remote(part.at[up_h, cols(xl)], rsin.at[j, top], rd_s, rs_r.at[j], left)
        remote(part.at[low_h, cols(xr)], rsin.at[j, low], rd_s, rs_r.at[j], right)

    def add_on(j):
        up_h, low_h = halves(j)
        drain(rin.at[j], ri_r.at[j])
        for h, rows, near, dev in ((0, up_h, xr, right), (1, low_h, xl, left)):
            sl = slice(h * HF, (h + 1) * HF)
            rout[j, sl] = (rin[j, sl].astype(F32) + part[rows, cols(near)].astype(F32)).astype(BF)
            half = pl.ds(h * HF, HF)
            remote(rout.at[j, half], rcin.at[j, half], rd_s, rc_r.at[j], dev)

    def finish(j):
        yy = src_plane(j)
        rows = plane_rows(yy)
        drain(rsin.at[j], rs_r.at[j])
        drain(rcin.at[j], rc_r.at[j])
        red[rows, :] = (
            rcin[j].astype(F32) + rsin[j].astype(F32) + part[rows, cols(x)].astype(F32)
        ).astype(BF)
        to_plane(red, rr, None, rt_s, rt_r.at[j], yy, j == 0)

    def combine(j):
        rows = plane_rows(dst_plane(j))
        drain(rr.at[rows], rt_r.at[j])
        got = tn(pm[rows, :], rr[rows, :])
        if j == 0:
            mg[...] = got
        else:
            mg[...] += got

    def weights_in(s):
        slot = s % 2
        if s >= 2:
            for w, o in ((0, dwg_o), (1, dwu_o)):
                pltpu.make_async_copy(
                    stage.at[slot, w], o.at[0, (s - 2) * 512 : (s - 1) * 512, :], stsem.at[slot, w]
                ).wait()

        def one(n, _):
            r = pl.ds(pl.multiple_of(n * 256, 256), 256)
            xt = xb[:, pl.ds(pl.multiple_of(s * 512 + n * 256, 256), 256)]
            stage[slot, 0, r, :] = tn(xt, gg[...]).astype(BF)
            stage[slot, 1, r, :] = tn(xt, ug[...]).astype(BF)
            return 0

        lax.fori_loop(0, 2, one, 0)
        for w, o in ((0, dwg_o), (1, dwu_o)):
            pltpu.make_async_copy(
                stage.at[slot, w], o.at[0, s * 512 : (s + 1) * 512, :], stsem.at[slot, w]
            ).start()

    def weights_out(s):
        slot, w = divmod(s, 2)
        o = (dwg_o, dwu_o)[w]
        pltpu.make_async_copy(
            stage.at[slot, w], o.at[0, (2 + slot) * 512 : (3 + slot) * 512, :], stsem.at[slot, w]
        ).wait()

        def one(n, _):
            r = pl.ds(pl.multiple_of(n * 256, 256), 256)
            stage[slot, w, r, :] = tn(act[:, r], yb[:, s * 512 : (s + 1) * 512]).astype(BF)
            return 0

        lax.fori_loop(0, 2, one, 0)
        pltpu.make_async_copy(
            stage.at[slot, w], dwd_o.at[0, :, s * 512 : (s + 1) * 512], stsem.at[slot, w]
        ).start()

    relay(1, 0)
    relay(1, 1)
    relay(1, 2)
    compute(0)
    relay(1, 3)
    compute(1)
    compute(2)
    add_on(0)
    compute(3)
    add_on(1)
    add_on(2)
    add_on(3)
    finish(0)
    finish(1)
    weights_in(0)
    weights_in(1)
    finish(2)
    weights_in(2)
    weights_in(3)
    combine(0)
    finish(3)
    combine(1)
    combine(2)
    weights_out(0)
    combine(3)

    for i in range(4):
        sl = slice(i * HD, (i + 1) * HD)
        m = mx[:, sl]
        scale = lax.rsqrt(jnp.mean(m * m, axis=-1, keepdims=True) + EPS)
        normed = m * scale
        hg = xg[:, :, sl].reshape(4 * TOK, HD).astype(F32) + mg[:, sl]
        ng = scale * (hg - normed * jnp.mean(hg * normed, axis=-1, keepdims=True))
        ngb = ng.astype(BF)
        bterm[i] = tn(xq[:, :, sl].reshape(4 * TOK, HD), ngb).astype(BF)
        qgs[:, :, sl] = nt(ngb, stb[i]).astype(BF).reshape(4, TOK, HD)
    for d in range(1, 4):
        zo = mod(z + d, 4)
        remote(bterm.at[zo], bz.at[z], bz_s, bz_r, (tm, zo * 4 + x))
    for d in range(1, 4):
        xo = mod(x + d, 4)
        remote(qgs.at[xo], qgb.at[x], qg_s, qg_r, (tm, z * 4 + xo))
    weights_out(1)
    drain(bz.at[pl.ds(0, 3)], bz_r)
    bz[z] = bterm[z]
    bspan[tm] = jnp.sum(bz[...].astype(F32), axis=0).astype(BF)

    def send_back_span(i, _):
        remote(bspan.at[tm], bspan.at[tm], bp_s, bp_r, (mod(tm + i, 8), e))
        return 0

    lax.fori_loop(1, 8, send_back_span, 0)
    weights_out(2)
    drain(bspan.at[pl.ds(0, 7)], bp_r)
    total = jnp.zeros((HD, HD), F32)
    for t in range(8):
        total = total + jnp.where(t >= tm, bspan[t].astype(F32), 0.0)
    bown[...] = total.astype(BF)

    def send_back(i, _):
        remote(bown, ball.at[e], bb_s, bb_r, (tm, mod(e + i, 16)))
        return 0

    lax.fori_loop(1, 16, send_back, 0)
    weights_out(3)
    drain(qgb.at[pl.ds(0, 3)], qg_r)
    qgb[x] = qgs[x]
    for b in range(4):
        qg_o[:, b * BC : (b + 1) * BC] = qgb[b]
    drain(ball.at[pl.ds(0, 15)], bb_r)
    ball[e] = bown[...]
    for eo in range(16):
        ball_o[(eo % 4) * 4 + eo // 4] = ball[eo]

    drain(srecv.at[pl.ds(0, 3)], st_s)
    drain(sxrecv.at[pl.ds(0, 3)], sx_s)
    drain(sspan.at[pl.ds(0, 7)], sp_s)
    drain(stb.at[pl.ds(0, 3)], sb_s)
    drain(rt.at[pl.ds(0, 3)], xt_s.at[0])
    drain(xg.at[pl.ds(0, 3)], xt_s.at[1])
    drain(xq.at[pl.ds(0, 3)], xt_s.at[2])
    for a in range(2):
        drain(small[a].at[pl.ds(0, 31 * G)], sl_s.at[a])
        for _ in range(3):
            drain(big[a].at[pl.ds(0, ROWS), pl.ds(0, BC)], mc_s.at[a])
    for _ in range(3):
        drain(red, rd_s)
    drain(red.at[pl.ds(0, 31 * G)], rt_s)
    drain(bz.at[pl.ds(0, 3)], bz_s)
    drain(bspan.at[pl.ds(0, 7)], bp_s)
    drain(ball.at[pl.ds(0, 15)], bb_s)
    drain(qgb.at[pl.ds(0, 3)], qg_s)
    for s in range(4):
        slot, w = divmod(s, 2)
        pltpu.make_async_copy(
            stage.at[slot, w], dwd_o.at[0, :, s * 512 : (s + 1) * 512], stsem.at[slot, w]
        ).wait()


def finish_kernel(qg, ball, k, v, dwg, dwu, dwd, qg_o, kg_o, vg_o, dwg_o, dwu_o, dwd_o):
    qg_o[...] = qg[...]
    dwg_o[...] = dwg[...].astype(F32)
    dwu_o[...] = dwu[...].astype(F32)
    dwd_o[...] = dwd[...].astype(F32)
    for i in range(16 // STEPS):
        sl = slice(i * HD, (i + 1) * HD)
        kg_o[:, sl] = nt(v[:, sl], ball[i]).astype(BF)
        vg_o[:, sl] = nn(k[:, sl], ball[i]).astype(BF)


def body(queries, keys, values, out_grad, expert_ids, combine_gates, gate_w, up_w, down_w):
    vm = pl.BlockSpec(memory_space=pltpu.VMEM)
    hbm = pl.BlockSpec(memory_space=pl.ANY)
    dma = pltpu.SemaphoreType.DMA
    scratch = [
        pltpu.VMEM((TOK, D), BF),
        pltpu.VMEM((TOK, D), BF),
        pltpu.VMEM((D, HID), BF),
        pltpu.VMEM((D, HID), BF),
        pltpu.VMEM((HID, D), BF),
        pltpu.VMEM((4, 4, HD, HD), BF),
        pltpu.VMEM((4, 4, HD, HD), BF),
        pltpu.VMEM((4, HD, HD), BF),
        pltpu.VMEM((4, HD, HD), BF),
        pltpu.VMEM((8, HD, HD), BF),
        pltpu.VMEM((4, HD, HD), BF),
        pltpu.VMEM((8, TOK), F32),
        pltpu.VMEM((4, 8, TOK), F32),
        pltpu.VMEM((4, TOK, BC), BF),
        pltpu.VMEM((4, TOK, BC), BF),
        pltpu.VMEM((ROWS, 4 * TOK), BF),
        pltpu.VMEM((ROWS, TOK), F32),
        pltpu.VMEM((ROWS, BC), BF),
        pltpu.VMEM((ROWS, BC), BF),
        pltpu.VMEM((ROWS, D), BF),
        pltpu.VMEM((ROWS, D), BF),
        pltpu.VMEM((4 * TOK, BC), F32),
        pltpu.VMEM((4 * TOK, BC), BF),
        pltpu.VMEM((ROWS, HID), BF),
        pltpu.VMEM((ROWS, HID), BF),
        pltpu.VMEM((ROWS, HID), BF),
        pltpu.VMEM((ROWS, D), BF),
        pltpu.VMEM((4, CH, BC), BF),
        pltpu.VMEM((4, CH, BC), BF),
        pltpu.VMEM((4, CH, BC), BF),
        pltpu.VMEM((4, CH, BC), BF),
        pltpu.VMEM((ROWS, BC), BF),
        pltpu.VMEM((ROWS, BC), BF),
        pltpu.VMEM((4 * TOK, BC), F32),
        pltpu.VMEM((2, 2, 512, 512), BF),
        pltpu.VMEM((4, HD, HD), BF),
        pltpu.VMEM((4, HD, HD), BF),
        pltpu.VMEM((8, HD, HD), BF),
        pltpu.VMEM((HD, HD), BF),
        pltpu.VMEM((16, HD, HD), BF),
        pltpu.VMEM((4, TOK, BC), BF),
        pltpu.VMEM((4, TOK, BC), BF),
        dma((2,)),
        dma((3,)),
        dma, dma, dma, dma, dma, dma, dma, dma,
        dma((3,)), dma((3,)),
        dma((2,)), dma((2, 4)),
        dma((2,)), dma((2, 4)), dma((2, 4)), dma((2, 4)),
        dma, dma((4,)), dma((4,)), dma((4,)),
        dma, dma((4,)),
        dma((2, 2)),
        dma, dma, dma, dma, dma, dma, dma, dma,
    ]
    tokens = jax.ShapeDtypeStruct((TOK, D), BF)
    grads_in = jax.ShapeDtypeStruct((1, D, HID), F32)
    grads_out = jax.ShapeDtypeStruct((1, HID, D), F32)
    query_grad, back, gate_g, up_g, down_g = pl.pallas_call(
        kernel,
        out_shape=(
            tokens,
            jax.ShapeDtypeStruct((16, HD, HD), BF),
            jax.ShapeDtypeStruct((1, D, HID), BF),
            jax.ShapeDtypeStruct((1, D, HID), BF),
            jax.ShapeDtypeStruct((1, HID, D), BF),
        ),
        in_specs=[vm] * 2 + [hbm] * 7,
        out_specs=(vm, vm, hbm, hbm, hbm),
        scratch_shapes=scratch,
        compiler_params=pltpu.CompilerParams(
            collective_id=0, has_side_effects=True, vmem_limit_bytes=61 * 2**20
        ),
    )(expert_ids.T, combine_gates.T, queries, keys, values, out_grad, gate_w, up_w, down_w)
    lanes = pl.BlockSpec((TOK, D // STEPS), lambda i: (0, i))
    wide = pl.BlockSpec((1, D // STEPS, HID), lambda i: (0, i, 0))
    tall = pl.BlockSpec((1, HID // STEPS, D), lambda i: (0, i, 0))
    return pl.pallas_call(
        finish_kernel,
        out_shape=(tokens, tokens, tokens, grads_in, grads_in, grads_out),
        grid=(STEPS,),
        in_specs=[lanes, pl.BlockSpec((16 // STEPS, HD, HD), lambda i: (i, 0, 0)), lanes, lanes, wide, wide, tall],
        out_specs=(lanes, lanes, lanes, wide, wide, tall),
    )(query_grad, back, keys, values, gate_g, up_g, down_g)


def solution(mesh):
    flat = P(("tm", "expert"), None)
    cube = P(("tm", "expert"), None, None)
    return jax.shard_map(
        body,
        mesh=mesh,
        in_specs=(flat,) * 6 + (cube,) * 3,
        out_specs=(flat,) * 3 + (cube,) * 3,
        check_vma=False,
    )
```
